256 devices in a mesh: grp: 8 (over x, core), cache: 32 (over y, z).
Axes of the slice: x: 4, y: 4, z: 8, core: 2. Of those that a mesh axis runs over, the one named last changes fastest.
Arguments:
- feature_rows: bfloat16 [262144, 768], P(('grp', 'cache'))
- request_ids: int32 [8192, 128], P(('grp', 'cache')), may hold values from 0 to 1023
- request_counts: int32 [256, 32], P(('grp', 'cache')), may hold values from 0 to 128, as said below
- self_ids: int32 [65536], P(('grp', 'cache')), may hold values from 0 to 1023
- blocks_one: int32 [512, 16], P(('grp', 'cache')), may hold values from 0 to 31
- mask_one: int32 [512, 16, 128, 128], P(('grp', 'cache')), may hold values from 0 to 1, as said below
- blocks_two: int32 [256, 24], P(('grp', 'cache')), may hold values from 0 to 63
- mask_two: int32 [256, 24, 128, 128], P(('grp', 'cache')), may hold values from 0 to 1, as said below
- w1_self: bfloat16 [768, 1024], replicated, may hold values from -0.21875 to 0.21875
- w1_neigh: bfloat16 [768, 1024], replicated, may hold values from -0.21875 to 0.21875
- w2_self: bfloat16 [1024, 1024], replicated, may hold values from -0.1875 to 0.1875
- w2_neigh: bfloat16 [1024, 1024], replicated, may hold values from -0.1875 to 0.1875
- bn_gain: float32 [1024], replicated, may hold values from 0.1 to 1.9
- bn_shift: float32 [1024], replicated, may hold values from -3 to 3
- bias_two: float32 [1024], replicated, may hold values from -3 to 3
Outputs:
- seed_states: bfloat16 [32768, 1024], P(('grp', 'cache'))
The draws below stay inside these ranges and needn't reach their ends.
Inputs may be any that keep to these rules, and one draw needn't show every extreme that they name: `request_ids`: row d * 32 + o lists local rows of owner o of device d's group. `request_counts`: some owners are asked for exactly 128 rows by every device of the group. `blocks_one`: blocks of the device's own input rows. `blocks_two`: blocks of the group table. `mask_one`: some rows are empty. `mask_two`: some rows are empty.
All inputs are finite; a program needn't handle non-finite values.
Results may differ from the reference program's by a relative error of at most 0.0046.
Values may be sent and summed in bfloat16 or wider, within the bound.
No kernel may reach another device: no remote copies, remote signals or barrier semaphores. Data moves between devices by JAX's collectives and lax.ppermute only.
A program may use at most 192 MiB of HBM per device.

```python
import math
import jax
import jax.numpy as jnp
from jax import lax

FEAT = 768
HID = 1024
BLK = 128
NB1 = 16
NB2 = 24
OWN_ROWS = 1024
IN_DEV = 4096
H1 = 256
S_DEV = 128
CAP = 128
N_GRP = 8
N_CACHE = 32
DEVICES = 256


def block_mask(key, block_rows, neighbours):
    key_limit, key_empty, key_cells = jax.random.split(key, 3)
    limits = jax.random.randint(key_limit, (block_rows, 1, BLK, 1), 3, 600)
    empty = jax.random.randint(key_empty, (block_rows, 1, BLK, 1), 0, 16) == 0
    limits = jnp.where(empty, 0, limits)
    cells = jax.random.randint(key_cells, (block_rows, neighbours, BLK, BLK), 0, 1024)
    return (cells < limits).astype(jnp.int32)


def draw_mask_one(key, part):
    key = jax.random.fold_in(key, 3)
    return block_mask(key, DEVICES * H1 // BLK, NB1)


def draw_mask_two(key, part):
    key = jax.random.fold_in(key, 5)
    return block_mask(key, DEVICES * S_DEV // BLK, NB2)


def draw_request_counts(key, part):
    key = jax.random.fold_in(key, 7)
    key_order, key_fill = jax.random.split(key)
    order = jax.random.permutation(key_order, N_CACHE)
    popular = order < max(1, N_CACHE // 8)
    drawn = jax.random.randint(key_fill, (DEVICES, N_CACHE), 0, CAP // 2 + 1)
    return jnp.where(popular[None, :], CAP, drawn).astype(jnp.int32)


def draw_feature_rows(key, part):
    key = jax.random.fold_in(key, 11)
    key_base, key_scale = jax.random.split(key, 2)
    total_rows = OWN_ROWS * DEVICES
    owner = (jnp.arange(total_rows) // OWN_ROWS).astype(jnp.float32)
    ramp = 0.6 + 1.2 * owner / max(DEVICES - 1, 1)
    row_scale = jnp.exp(jax.random.uniform(key_scale, (total_rows, 1), minval=math.log(0.3), maxval=math.log(3.0)))
    base = jax.random.normal(key_base, (total_rows, FEAT))
    return (base * ramp[:, None] * row_scale).astype(jnp.bfloat16)


def with_ends(drawn, key, least, high):
    extent = drawn.shape
    place = [jax.random.randint(jax.random.fold_in(key, axis), (), 0, extent[axis]) for axis in range(len(extent))]
    drawn = drawn.at[tuple(place)].set(least)
    longest = extent.index(max(extent))
    place[longest] = (place[longest] + 1) % extent[longest]
    return drawn.at[tuple(place)].set(high)


def normal_values(key, dims, spread, limit, kind=jnp.bfloat16):
    return jnp.clip(spread * jax.random.normal(key, dims, jnp.float32), -limit, limit).astype(kind)


def setup_inputs(seed: int = 0) -> dict:
    key_list = jax.random.split(jax.random.key(seed), 16)
    return {
        "feature_rows": draw_feature_rows(jax.random.fold_in(key_list[15], 71), 0),
        "request_ids": with_ends(jax.random.randint(key_list[1], (DEVICES * N_CACHE, CAP), 0, OWN_ROWS), jax.random.fold_in(key_list[1], 1), 0, OWN_ROWS - 1).astype(jnp.int32),
        "request_counts": draw_request_counts(jax.random.fold_in(key_list[15], 71), 0),
        "self_ids": with_ends(jax.random.randint(key_list[3], (DEVICES * H1,), 0, OWN_ROWS), jax.random.fold_in(key_list[3], 1), 0, OWN_ROWS - 1).astype(jnp.int32),
        "blocks_one": with_ends(jax.random.randint(key_list[4], (DEVICES * H1 // BLK, NB1), 0, IN_DEV // BLK), jax.random.fold_in(key_list[4], 1), 0, (IN_DEV // BLK) - 1).astype(jnp.int32),
        "mask_one": draw_mask_one(jax.random.fold_in(key_list[15], 71), 0),
        "blocks_two": with_ends(jax.random.randint(key_list[6], (DEVICES * S_DEV // BLK, NB2), 0, H1 * N_CACHE // BLK), jax.random.fold_in(key_list[6], 1), 0, (H1 * N_CACHE // BLK) - 1).astype(jnp.int32),
        "mask_two": draw_mask_two(jax.random.fold_in(key_list[15], 71), 0),
        "w1_self": normal_values(key_list[8], (FEAT, HID), FEAT ** -0.5, 0.21875),
        "w1_neigh": normal_values(key_list[9], (FEAT, HID), FEAT ** -0.5, 0.21875),
        "w2_self": normal_values(key_list[10], (HID, HID), HID ** -0.5, 0.1875),
        "w2_neigh": normal_values(key_list[11], (HID, HID), HID ** -0.5, 0.1875),
        "bn_gain": jnp.clip(1.0 + 0.18 * jax.random.normal(key_list[12], (HID,), jnp.float32), 0.1, 1.9),
        "bn_shift": normal_values(key_list[13], (HID,), 0.5, 3.0, jnp.float32),
        "bias_two": normal_values(key_list[14], (HID,), 0.5, 3.0, jnp.float32),
    }


epsilon = 1e-05

def reference(feature_rows, request_ids, request_counts, self_ids, blocks_one, mask_one, blocks_two, mask_two, w1_self, w1_neigh, w2_self, w2_neigh, bn_gain, bn_shift, bias_two):
    ask_all = request_ids.reshape(DEVICES, N_CACHE, CAP)
    self_all = self_ids.reshape(DEVICES, H1)
    blocks_all = blocks_one.reshape(DEVICES, H1 // BLK, NB1)
    mask_all = mask_one.reshape(DEVICES, H1 // BLK, NB1, BLK, BLK)
    devices = jnp.arange(DEVICES, dtype=jnp.int32)

    def first_layer(packed):
        device, asked, counts, selves, blocks, mask = packed
        group = device // N_CACHE
        owners = jnp.arange(N_CACHE, dtype=jnp.int32)
        global_rows = (group * N_CACHE + owners[:, None]) * OWN_ROWS + asked
        inputs = feature_rows[global_rows.reshape(-1)]
        projected = jnp.dot(inputs, w1_neigh, preferred_element_type=jnp.float32).astype(jnp.bfloat16)
        usable = (jnp.arange(CAP, dtype=jnp.int32)[None, :] < counts[:, None]).reshape(-1)
        projected = jnp.where(usable[:, None], projected, jnp.zeros_like(projected))
        picked = projected.reshape(-1, BLK, HID)[blocks]
        summed = jnp.einsum('bkij,bkjh->bih', mask.astype(jnp.float32), picked.astype(jnp.float32))
        usable_blocks = usable.astype(jnp.int32).reshape(-1, BLK)[blocks]
        degree = lax.optimization_barrier(jnp.sum(mask * usable_blocks[:, :, None, :], axis=(1, 3))).astype(jnp.float32)
        neigh = (summed / jnp.maximum(degree, 1.0)[:, :, None]).reshape(-1, HID)
        own_rows = feature_rows[device * OWN_ROWS + selves]
        return jnp.dot(own_rows, w1_self, preferred_element_type=jnp.float32) + neigh
    pre = lax.map(first_layer, (devices, ask_all, request_counts, self_all, blocks_all, mask_all))
    row_total = DEVICES * H1
    batch_mean = lax.optimization_barrier(jnp.sum(pre, axis=(0, 1))) / row_total
    batch_msq = lax.optimization_barrier(jnp.sum(pre * pre, axis=(0, 1))) / row_total
    batch_var = batch_msq - batch_mean * batch_mean
    normed = bn_gain * (pre - batch_mean) / jnp.sqrt(batch_var + epsilon) + bn_shift
    layer_one = jnp.maximum(normed, 0.0).astype(jnp.bfloat16)
    table = layer_one.reshape(N_GRP, N_CACHE * H1 // BLK, BLK, HID)
    blocks_seed = blocks_two.reshape(DEVICES, S_DEV // BLK, NB2)
    mask_seed = mask_two.reshape(DEVICES, S_DEV // BLK, NB2, BLK, BLK)

    def second_layer(packed):
        device, blocks, mask = packed
        group_table = table[device // N_CACHE]
        picked = group_table[blocks]
        summed = jnp.einsum('bkij,bkjh->bih', mask.astype(jnp.float32), picked.astype(jnp.float32))
        degree = lax.optimization_barrier(jnp.sum(mask, axis=(1, 3))).astype(jnp.float32)
        neigh_two = (summed / jnp.maximum(degree, 1.0)[:, :, None]).reshape(S_DEV, HID).astype(jnp.bfloat16)
        own_states = layer_one[device, :S_DEV]
        result = jnp.dot(own_states, w2_self, preferred_element_type=jnp.float32)
        result = result + jnp.dot(neigh_two, w2_neigh, preferred_element_type=jnp.float32) + bias_two
        return result.astype(jnp.bfloat16)
    seed_states = lax.map(second_layer, (devices, blocks_seed, mask_seed))
    return seed_states.reshape(DEVICES * S_DEV, HID)
```

```python
import functools

import jax
import jax.numpy as jnp
from jax import lax
from jax.experimental import pallas as pl
from jax.experimental.pallas import tpu as pltpu
from jax.sharding import PartitionSpec as P

BLK = 128
FEAT = 768
HID = 1024
NB1 = 16
NB2 = 24
NY = 4
NZ = 8
ROWS = 65536.0
EPS = 1e-05

BF = jnp.bfloat16
F32 = jnp.float32

VM = pl.BlockSpec(memory_space=pltpu.VMEM)
SM = pl.BlockSpec(memory_space=pltpu.SMEM)

CHUNKS = ((4, 5), (3, 6), (2, 7), (1,), (0,))


def call(kernel, outs, ins, scratch=(), flops=0, nbytes=0, vmem=40):
    return pl.pallas_call(
        kernel,
        out_shape=outs,
        in_specs=ins,
        out_specs=jax.tree.map(lambda _: VM, outs),
        scratch_shapes=scratch,
        cost_estimate=pl.CostEstimate(flops=flops, bytes_accessed=nbytes, transcendentals=0),
        compiler_params=pltpu.CompilerParams(vmem_limit_bytes=vmem * 1024 * 1024),
    )


def sds(shape, dtype):
    return jax.ShapeDtypeStruct(shape, dtype)


def adj_one_kernel(me, blocks, counts, mask, *refs):
    outs, deg, acc = refs[:NZ], refs[NZ], refs[NZ + 1]
    my, mz = me[0] >> 3, me[0] & 7
    acc[...] = jnp.zeros_like(acc)
    lane = lax.broadcasted_iota(jnp.int32, (BLK, BLK), 1)
    for b in range(2):

        def step(k, total, b=b):
            o = blocks[b, k]
            rel = ((mz - (o & 7)) & 7) * NY + ((my - (o >> 3)) & 3)
            m = jnp.where(lane < counts[0, o], mask[b, k], 0).astype(F32)
            acc[rel, b * BLK : (b + 1) * BLK, :] += m
            return total + m

        total = lax.fori_loop(0, NB1, step, jnp.zeros((BLK, BLK), F32), unroll=4)
        deg[b * BLK : (b + 1) * BLK, :] = jnp.maximum(jnp.sum(total, axis=1, keepdims=True), 1.0)
    for j in range(NZ):
        for dy in range(NY):
            outs[j][:, dy * BLK : (dy + 1) * BLK] = acc[j * NY + dy].astype(BF)


def adj_two_kernel(me, blocks, mask, *refs):
    outs, deg, acc = refs[:NY], refs[NY], refs[NY + 1]
    my, mz = me[0] >> 3, me[0] & 7
    acc[...] = jnp.zeros_like(acc)

    def step(k, total):
        c = blocks[0, k]
        o = c >> 1
        rel = ((my - (o >> 3)) & 3) * 16 + ((mz - (o & 7)) & 7) * 2 + (c & 1)
        m = mask[0, k].astype(F32)
        acc[rel] += m
        return total + m

    total = lax.fori_loop(0, NB2, step, jnp.zeros((BLK, BLK), F32), unroll=4)
    deg[...] = jnp.maximum(jnp.sum(total, axis=1, keepdims=True), 1.0)
    for dy in range(NY):
        for t in range(16):
            outs[dy][:, t * BLK : (t + 1) * BLK] = acc[dy * 16 + t].astype(BF)


def pick_kernel(js, me, ids, table, *outs):
    my, mz = me[0] >> 3, me[0] & 7
    iota = lax.broadcasted_iota(jnp.int32, (BLK, HID), 1).astype(F32)
    for dy in range(NY):
        hots = []
        for j in js:
            r = ((my + dy) & 3) * NZ + ((mz + j) & 7)
            row = ids[pl.ds(r, 1), :].astype(F32)
            col = jnp.broadcast_to(row, (BLK, BLK)).T
            wide = jnp.concatenate([col] * (HID // BLK), axis=1)
            hots.append(jnp.where(wide == iota, 1.0, 0.0).astype(BF))
        hot = jnp.concatenate(hots, axis=0) if len(hots) > 1 else hots[0]
        outs[dy][...] = jnp.dot(hot, table[...], preferred_element_type=F32).astype(BF)


def partial_sum(adj, rows, t):
    x = jnp.concatenate([r[t * BLK : (t + 1) * BLK, :] for r in rows], axis=0)
    return jnp.dot(adj[...], x, preferred_element_type=F32)


def step_kernel(terms, carries, *refs):
    adjs, refs = refs[:terms], refs[terms:]
    rows, refs = refs[:NY], refs[NY:]
    ins, outs = (refs[:terms], refs[terms:]) if carries else (None, refs)
    for t in range(terms):
        s = partial_sum(adjs[t], rows, t)
        if carries:
            s = s + ins[t][...].astype(F32)
        outs[t][...] = s.astype(BF)


def pre_kernel(adj, x0, x1, x2, x3, right, left, deg, own, w_neigh, pre, pre16, stats):
    s = partial_sum(adj, (x0, x1, x2, x3), 0) + right[...].astype(F32) + left[...].astype(F32)
    high = s.astype(BF)
    low = (s - high.astype(F32)).astype(BF)
    both = jnp.dot(jnp.concatenate([high, low], axis=0), w_neigh[...], preferred_element_type=F32)
    p = own[...] + (both[: 2 * BLK] + both[2 * BLK :]) / deg[...]
    pre[...] = p
    pre16[...] = p.astype(BF)
    stats[0:1, :] = jnp.sum(p, axis=0, keepdims=True)
    stats[1:2, :] = jnp.sum(p * p, axis=0, keepdims=True)


def norm_terms(stats, gain, shift):
    mean = stats[0:1, :] / ROWS
    var = stats[1:2, :] / ROWS - mean * mean
    scale = gain[...] / jnp.sqrt(var + EPS)
    return scale, shift[...] - scale * mean


def states(p, scale, offset):
    return jnp.maximum(p.astype(F32) * scale + offset, 0.0).astype(BF)


def peers_kernel(stats, gain, shift, m0, m1, m2, m3, b0, b1, b2, b3, b5, b6, b7, pre, w_self, bias, acc, own):
    scale, offset = norm_terms(stats, gain, shift)
    for n, (r, b) in enumerate(((0, b0), (1, b1), (7, b7), (2, b2), (6, b6), (3, b3), (5, b5))):
        h = states(b[...], scale, offset)
        m = jnp.concatenate([x[:, r * 256 : (r + 1) * 256] for x in (m0, m1, m2, m3)], axis=0)
        term = jnp.dot(m, h, preferred_element_type=F32)
        if n == 0:
            acc[...] = term
        else:
            acc[...] += term
    h = states(pre[:BLK, :], scale, offset)
    own[...] = jnp.dot(h, w_self[...], preferred_element_type=F32) + bias[...]


def last_peers_kernel(stats, gain, shift, m0, m1, m2, m3, b4a, b4b, acc, p0, p1, p2, p3):
    scale, offset = norm_terms(stats, gain, shift)
    h = jnp.concatenate([states(b4a[...], scale, offset), states(b4b[...], scale, offset)], axis=0)
    for dy, (m, out) in enumerate(((m0, p0), (m1, p1), (m2, p2), (m3, p3))):
        s = acc[dy * BLK : (dy + 1) * BLK, :] + jnp.dot(m[:, 1024:1280], h, preferred_element_type=F32)
        out[...] = s.astype(out.dtype)


def out_kernel(own, p0, p1, p2, p3, deg, w, out):
    s = p0[...] + p1[...].astype(F32) + p2[...].astype(F32) + p3[...].astype(F32)
    n = (s / deg[...]).astype(BF)
    out[...] = (own[...] + jnp.dot(n, w[...], preferred_element_type=F32)).astype(BF)


def along_y(x, k):
    return lax.ppermute(x, "cache", [(y * NZ + z, (y + k) % NY * NZ + z) for y in range(NY) for z in range(NZ)])


def along_z(x, k):
    return lax.ppermute(x, "cache", [(y * NZ + z, y * NZ + (z + k) % NZ) for y in range(NY) for z in range(NZ)])


def body(
    feature_rows,
    request_ids,
    request_counts,
    self_ids,
    blocks_one,
    mask_one,
    blocks_two,
    mask_two,
    w1_self,
    w1_neigh,
    w2_self,
    w2_neigh,
    bn_gain,
    bn_shift,
    bias_two,
):
    me = lax.axis_index("cache").astype(jnp.int32).reshape(1)
    gain, shift, bias = (v.reshape(1, HID) for v in (bn_gain, bn_shift, bias_two))

    asked = lax.all_to_all(request_ids, "cache", split_axis=0, concat_axis=0, tiled=True)

    *adj, deg_one = call(
        adj_one_kernel,
        [sds((2 * BLK, NY * BLK), BF)] * NZ + [sds((2 * BLK, 1), F32)],
        [SM, SM, SM, VM],
        [pltpu.VMEM((NZ * NY, 2 * BLK, BLK), F32)],
        flops=1 << 22,
        nbytes=4 << 20,
    )(me, blocks_one, request_counts, mask_one)
    adj_here = {j: along_z(adj[j], -j) if j else adj[0] for j in (4, 5, 3, 6, 2, 7, 1, 0)}

    rows_here = []
    for js in CHUNKS:
        rows = call(
            functools.partial(pick_kernel, js),
            [sds((len(js) * BLK, FEAT), BF)] * NY,
            [SM, VM, VM],
            flops=2 * 4 * len(js) * BLK * 1024 * FEAT,
            nbytes=3 << 20,
        )(me, asked, feature_rows)
        rows_here.append([along_y(r, dy) if dy else r for dy, r in enumerate(rows)])

    own = jnp.dot(feature_rows[self_ids], w1_self, preferred_element_type=F32)

    sums = None
    for js, rows in zip(CHUNKS[:4], rows_here[:4]):
        terms = len(js)
        out = call(
            functools.partial(step_kernel, terms, sums is not None),
            [sds((2 * BLK, FEAT), BF)] * terms,
            [VM] * (terms + NY + (terms if sums else 0)),
            flops=2 * terms * 256 * 512 * FEAT,
            nbytes=terms * 2 << 20,
        )(*[adj_here[j] for j in js], *rows, *((sums[:terms]) if sums else ()))
        sums = [along_z(s, 1 - 2 * t) for t, s in enumerate(out)] + (sums[1:] if terms == 1 else [])

    pre, pre16, stats = call(
        pre_kernel,
        [sds((2 * BLK, HID), F32), sds((2 * BLK, HID), BF), sds((2, HID), F32)],
        [VM] * 10,
        flops=2 * 256 * 512 * FEAT + 4 * 256 * FEAT * HID,
        nbytes=6 << 20,
    )(adj_here[0], *rows_here[4], *sums, deg_one, own, w1_neigh)

    blocks = {0: pre16}
    for i in range(1, 4):
        blocks[i] = along_z(blocks[i - 1], 1)
        blocks[8 - i] = along_z(blocks[(9 - i) % 8], -1)
    far_a = along_z(blocks[3][:BLK], 1)
    far_b = along_z(blocks[5][BLK:], -1)

    for k in (1, 2, 4):
        stats = stats + lax.ppermute(stats, "grp", [(i, i ^ k) for i in range(8)])
    for k in (8, 16, 1, 2, 4):
        stats = stats + lax.ppermute(stats, "cache", [(i, i ^ k) for i in range(32)])

    *adj_two, deg_two = call(
        adj_two_kernel,
        [sds((BLK, 16 * BLK), BF)] * NY + [sds((BLK, 1), F32)],
        [SM, SM, VM],
        [pltpu.VMEM((NY * 16, BLK, BLK), F32)],
        flops=1 << 22,
        nbytes=4 << 20,
    )(me, blocks_two, mask_two)
    peers = [along_y(m, -dy) if dy else m for dy, m in enumerate(adj_two)]

    acc, own_out = call(
        peers_kernel,
        [sds((NY * BLK, HID), F32), sds((BLK, HID), F32)],
        [VM] * 17,
        flops=2 * 512 * 1792 * HID,
        nbytes=12 << 20,
    )(stats, gain, shift, *peers, *[blocks[r] for r in (0, 1, 2, 3, 5, 6, 7)], pre, w2_self, bias)
    parts = call(
        last_peers_kernel,
        [sds((BLK, HID), F32)] + [sds((BLK, HID), BF)] * 3,
        [VM] * 10,
        flops=2 * 512 * 256 * HID,
        nbytes=4 << 20,
    )(stats, gain, shift, *peers, far_a, far_b, acc)
    parts = [along_y(p, dy) if dy else p for dy, p in enumerate(parts)]
    return call(
        out_kernel,
        sds((BLK, HID), BF),
        [VM] * 7,
        flops=2 * BLK * HID * HID,
        nbytes=5 << 20,
    )(own_out, *parts, deg_two, w2_neigh)


def solution(mesh):
    rows = P(("grp", "cache"))
    in_specs = (rows,) * 8 + (P(),) * 7
    return jax.shard_map(body, mesh=mesh, in_specs=in_specs, out_specs=rows, check_vma=False)
```

```python
import functools
import math

import jax
import jax.numpy as jnp
from jax import lax
from jax.experimental import pallas as pl
from jax.experimental.pallas import tpu as pltpu
from jax.sharding import PartitionSpec as P

BLK = 128
FEAT = 768
HID = 1024
NB1 = 16
NB2 = 24
NY = 4
NZ = 8
ROWS = 65536.0
EPS = 1e-05

BF = jnp.bfloat16
F32 = jnp.float32

VM = pl.BlockSpec(memory_space=pltpu.VMEM)
SM = pl.BlockSpec(memory_space=pltpu.SMEM)

CHUNKS = ((4, 3, 5), (2, 6, 1, 7, 0))
HALF = FEAT // 2


def nbytes_of(x):
    return math.prod(x.shape) * x.dtype.itemsize


def call(kernel, outs, scalars, args, scratch=(), flops=0):
    held = sum(nbytes_of(x) for x in (*args, *outs, *scratch))
    mib = held * 3 // (2 << 20) + 4
    return pl.pallas_call(
        kernel,
        out_shape=outs,
        in_specs=[SM] * len(scalars) + [VM] * len(args),
        out_specs=[VM] * len(outs),
        scratch_shapes=[pltpu.VMEM(x.shape, x.dtype) for x in scratch],
        cost_estimate=pl.CostEstimate(flops=flops, bytes_accessed=held, transcendentals=0),
        compiler_params=pltpu.CompilerParams(vmem_limit_bytes=mib * 1024 * 1024),
    )(*scalars, *args)


def sds(shape, dtype):
    return jax.ShapeDtypeStruct(shape, dtype)


def adj_one_kernel(me, blocks, counts, mask, out, deg, acc):
    my = me[0] >> 3
    acc[...] = jnp.zeros_like(acc)
    lane = lax.broadcasted_iota(jnp.int32, (BLK, BLK), 1)
    for b in range(2):

        def step(k, total, b=b):
            o = blocks[b, k]
            rel = (o & 7) * NY + ((my - (o >> 3)) & 3)
            m = jnp.where(lane < counts[0, o], mask[b, k], 0).astype(F32)
            acc[rel, b * BLK : (b + 1) * BLK, :] += m
            return total + m

        total = lax.fori_loop(0, NB1, step, jnp.zeros((BLK, BLK), F32), unroll=4)
        deg[b * BLK : (b + 1) * BLK, :] = jnp.maximum(jnp.sum(total, axis=1, keepdims=True), 1.0)
    for j in range(NZ):
        for dy in range(NY):
            out[j, :, dy * BLK : (dy + 1) * BLK] = acc[j * NY + dy].astype(BF)


def adj_two_kernel(me, blocks, mask, out, deg, acc):
    mz = me[0] & 7
    acc[...] = jnp.zeros_like(acc)

    def step(k, total):
        c = blocks[0, k]
        o = c >> 1
        rel = (o >> 3) * 16 + ((mz - (o & 7)) & 7) * 2 + (c & 1)
        m = mask[0, k].astype(F32)
        acc[rel] += m
        return total + m

    total = lax.fori_loop(0, NB2, step, jnp.zeros((BLK, BLK), F32), unroll=4)
    deg[...] = jnp.maximum(jnp.sum(total, axis=1, keepdims=True), 1.0)
    for y in range(NY):
        for t in range(16):
            out[y, :, t * BLK : (t + 1) * BLK] = acc[y * 16 + t].astype(BF)


def pick_kernel(js, me, ids, table, *outs):
    my, mz = me[0] >> 3, me[0] & 7
    iota = lax.broadcasted_iota(jnp.int32, (BLK, HID), 1).astype(F32)
    for dy in range(NY):
        hots = []
        for j in js:
            r = ((my + dy) & 3) * NZ + ((mz + j) & 7)
            col = jnp.broadcast_to(ids[pl.ds(r, 1), :].astype(F32), (BLK, BLK)).T
            wide = jnp.concatenate([col] * (HID // BLK), axis=1)
            hots.append(jnp.where(wide == iota, 1.0, 0.0).astype(BF))
        hot = jnp.concatenate(hots, axis=0) if len(hots) > 1 else hots[0]
        outs[dy][...] = jnp.dot(hot, table[...], preferred_element_type=F32).astype(BF)


def partial_sum(me, adj, rows, j, t):
    x = jnp.concatenate([r[t * BLK : (t + 1) * BLK, :] for r in rows], axis=0)
    return jnp.dot(adj[((me[0] & 7) + j) & 7], x, preferred_element_type=F32)


def far_kernel(me, adj, x0, x1, x2, x3, right, left):
    s = partial_sum(me, adj, (x0, x1, x2, x3), 4, 0)
    right[...] = s[:, :HALF].astype(BF)
    left[...] = s[:, HALF:].astype(BF)


def local_kernel(js, t0, me, adj, *refs):
    rows, outs = refs[:NY], refs[NY:]
    for n, j in enumerate(js):
        outs[n][...] = partial_sum(me, adj, rows, j, t0 + n)


def first_add_kernel(p, q, r, l, right, left):
    right[:, :HALF] = (p[:, :HALF] + r[...].astype(F32)).astype(BF)
    right[:, HALF:] = p[:, HALF:].astype(BF)
    left[:, :HALF] = q[:, :HALF].astype(BF)
    left[:, HALF:] = (q[:, HALF:] + l[...].astype(F32)).astype(BF)


def add_kernel(p, q, r, l, right, left):
    right[...] = (p[...] + r[...].astype(F32)).astype(BF)
    left[...] = (q[...] + l[...].astype(F32)).astype(BF)


def pre_kernel(here, right, left, deg, own, w_neigh, pre, pre16, stats):
    s = here[...] + right[...].astype(F32) + left[...].astype(F32)
    high = s.astype(BF)
    low = (s - high.astype(F32)).astype(BF)
    both = jnp.dot(jnp.concatenate([high, low], axis=0), w_neigh[...], preferred_element_type=F32)
    p = own[...] + (both[: 2 * BLK] + both[2 * BLK :]) / deg[...]
    pre[...] = p
    pre16[...] = p.astype(BF)
    stats[0:1, :] = jnp.sum(p, axis=0, keepdims=True)
    stats[1:2, :] = jnp.sum(p * p, axis=0, keepdims=True)


def norm_terms(stats, gain, shift):
    mean = stats[0:1, :] / ROWS
    var = stats[1:2, :] / ROWS - mean * mean
    scale = gain[...] / jnp.sqrt(var + EPS)
    return scale, shift[...] - scale * mean


def states(p, scale, offset):
    return jnp.maximum(p.astype(F32) * scale + offset, 0.0).astype(BF)


def peers_kernel(stats, gain, shift, adj, b0, b1, b2, b3, b5, b6, b7, pre, w_self, bias, acc, own):
    scale, offset = norm_terms(stats, gain, shift)
    for n, (r, b) in enumerate(((0, b0), (1, b1), (7, b7), (2, b2), (6, b6), (3, b3), (5, b5))):
        h = states(b[...], scale, offset)
        m = jnp.concatenate([adj[y, :, r * 256 : (r + 1) * 256] for y in range(NY)], axis=0)
        term = jnp.dot(m, h, preferred_element_type=F32)
        if n == 0:
            acc[...] = term
        else:
            acc[...] += term
    h = states(pre[:BLK, :], scale, offset)
    own[...] = jnp.dot(h, w_self[...], preferred_element_type=F32) + bias[...]


def last_peers_kernel(me, stats, gain, shift, adj, b4a, b4b, acc, *outs):
    my = me[0] >> 3
    scale, offset = norm_terms(stats, gain, shift)
    h = jnp.concatenate([states(b4a[...], scale, offset), states(b4b[...], scale, offset)], axis=0)
    for dy, out in enumerate(outs):
        y = (my + dy) & 3
        s = jnp.dot(adj[y, :, 1024:1280], h, preferred_element_type=F32)
        s = s + acc[pl.ds(pl.multiple_of(y * BLK, BLK), BLK), :]
        out[...] = s.astype(out.dtype)


def out_kernel(own, p0, p1, p2, p3, deg, w, out):
    s = p0[...] + p1[...].astype(F32) + p2[...].astype(F32) + p3[...].astype(F32)
    n = (s / deg[...]).astype(BF)
    out[...] = (own[...] + jnp.dot(n, w[...], preferred_element_type=F32)).astype(BF)


def along_y(x, k):
    return lax.ppermute(x, "cache", [(y * NZ + z, (y + k) % NY * NZ + z) for y in range(NY) for z in range(NZ)])


def along_z(x, k):
    return lax.ppermute(x, "cache", [(y * NZ + z, y * NZ + (z + k) % NZ) for y in range(NY) for z in range(NZ)])


def body(
    feature_rows,
    request_ids,
    request_counts,
    self_ids,
    blocks_one,
    mask_one,
    blocks_two,
    mask_two,
    w1_self,
    w1_neigh,
    w2_self,
    w2_neigh,
    bn_gain,
    bn_shift,
    bias_two,
):
    me = lax.axis_index("cache").astype(jnp.int32).reshape(1)
    gain, shift, bias = (v.reshape(1, HID) for v in (bn_gain, bn_shift, bias_two))

    asked = lax.all_to_all(request_ids, "cache", split_axis=0, concat_axis=0, tiled=True)

    adj, deg_one = call(
        adj_one_kernel,
        [sds((NZ, 2 * BLK, NY * BLK), BF), sds((2 * BLK, 1), F32)],
        [me, blocks_one, request_counts],
        [mask_one],
        [sds((NZ * NY, 2 * BLK, BLK), F32)],
        flops=1 << 22,
    )
    rings = [[y * NZ + z for z in range(NZ)] for y in range(NY)]
    adj = lax.all_to_all(adj, "cache", split_axis=0, concat_axis=0, tiled=True, axis_index_groups=rings)

    rows_here = []
    for js in CHUNKS:
        rows = call(
            functools.partial(pick_kernel, js),
            [sds((len(js) * BLK, FEAT), BF)] * NY,
            [me],
            [asked, feature_rows],
            flops=2 * 4 * len(js) * BLK * 1024 * FEAT,
        )
        rows_here.append([along_y(r, dy) if dy else r for dy, r in enumerate(rows)])
    first, second = rows_here

    own = jnp.dot(feature_rows[self_ids], w1_self, preferred_element_type=F32)

    adj_two, deg_two = call(
        adj_two_kernel,
        [sds((NY, BLK, 16 * BLK), BF), sds((BLK, 1), F32)],
        [me, blocks_two],
        [mask_two],
        [sds((NY * 16, BLK, BLK), F32)],
        flops=1 << 22,
    )
    adj_two, *second = lax.optimization_barrier((adj_two, *second))
    rings = [[y * NZ + z for y in range(NY)] for z in range(NZ)]
    adj_two = lax.all_to_all(adj_two, "cache", split_axis=0, concat_axis=0, tiled=True, axis_index_groups=rings)

    def local(js, t0, rows):
        return call(
            functools.partial(local_kernel, js, t0),
            [sds((2 * BLK, FEAT), F32)] * len(js),
            [me],
            [adj, *rows],
            flops=2 * len(js) * 256 * 512 * FEAT,
        )

    right, left = call(
        far_kernel, [sds((2 * BLK, HALF), BF)] * 2, [me], [adj, *first], flops=2 * 256 * 512 * FEAT
    )
    near = local((3, 5), 1, first)
    rest = local(CHUNKS[1], 0, second)
    right, left = along_z(right, 1), along_z(left, -1)
    for n, terms in enumerate((near, rest[:2], rest[2:4])):
        right, left = call(
            add_kernel if n else first_add_kernel,
            [sds((2 * BLK, FEAT), BF)] * 2,
            [],
            [*terms, right, left],
            flops=1 << 20,
        )
        right, left = along_z(right, 1), along_z(left, -1)

    pre, pre16, stats = call(
        pre_kernel,
        [sds((2 * BLK, HID), F32), sds((2 * BLK, HID), BF), sds((2, HID), F32)],
        [],
        [rest[4], right, left, deg_one, own, w1_neigh],
        flops=4 * 256 * FEAT * HID,
    )

    def add_over(st, axis, *ks):
        n = lax.axis_size(axis)
        return sum((lax.ppermute(st, axis, [(i, i ^ k) for i in range(n)]) for k in ks), st)

    b1, b7 = along_z(pre16, 1), along_z(pre16, -1)
    stats = add_over(add_over(stats, "grp", 1), "grp", 2, 4, 6)
    b1, b7, stats, adj_two = lax.optimization_barrier((b1, b7, stats, adj_two))
    b2, b6 = along_z(b1, 1), along_z(b7, -1)
    stats = add_over(add_over(stats, "cache", 8, 16, 24), "cache", 1, 2, 3)
    b2, b6, stats = lax.optimization_barrier((b2, b6, stats))
    b3, b5 = along_z(b2, 1), along_z(b6, -1)
    stats = add_over(stats, "cache", 4)
    b3, b5, stats = lax.optimization_barrier((b3, b5, stats))
    far_a = along_z(b3[:BLK], 1)
    far_b = along_z(b5[BLK:], -1)

    acc, own_out = call(
        peers_kernel,
        [sds((NY * BLK, HID), F32), sds((BLK, HID), F32)],
        [],
        [stats, gain, shift, adj_two, pre16, b1, b2, b3, b5, b6, b7, pre, w2_self, bias],
        flops=2 * 512 * 1792 * HID,
    )
    parts = call(
        last_peers_kernel,
        [sds((BLK, HID), F32)] + [sds((BLK, HID), BF)] * 3,
        [me],
        [stats, gain, shift, adj_two, far_a, far_b, acc],
        flops=2 * 512 * 256 * HID,
    )
    parts = [along_y(p, dy) if dy else p for dy, p in enumerate(parts)]
    return call(
        out_kernel,
        [sds((BLK, HID), BF)],
        [],
        [own_out, *parts, deg_two, w2_neigh],
        flops=2 * BLK * HID * HID,
    )[0]


def solution(mesh):
    rows = P(("grp", "cache"))
    in_specs = (rows,) * 8 + (P(),) * 7
    return jax.shard_map(body, mesh=mesh, in_specs=in_specs, out_specs=rows, check_vma=False)
```

```python
import functools
import math

import jax
import jax.numpy as jnp
from jax import lax
from jax.experimental import pallas as pl
from jax.experimental.pallas import tpu as pltpu
from jax.sharding import PartitionSpec as P

BLK = 128
FEAT = 768
HID = 1024
NB1 = 16
NB2 = 24
NY = 4
NZ = 8
ROWS = 65536.0
EPS = 1e-05

BF = jnp.bfloat16
F32 = jnp.float32

VM = pl.BlockSpec(memory_space=pltpu.VMEM)
SM = pl.BlockSpec(memory_space=pltpu.SMEM)
HB = pl.BlockSpec(memory_space=pltpu.HBM)

CHUNKS = ((4, 3, 5), (2, 6, 1, 7, 0))
HALF = FEAT // 2


def nbytes_of(x):
    return math.prod(x.shape) * x.dtype.itemsize


def call(kernel, outs, scalars, args, scratch=(), flops=0):
    held = sum(nbytes_of(x) for x in (*args, *outs, *scratch))
    mib = held * 3 // (2 << 20) + 4
    return pl.pallas_call(
        kernel,
        out_shape=outs,
        in_specs=[SM] * len(scalars) + [VM] * len(args),
        out_specs=[VM] * len(outs),
        scratch_shapes=[pltpu.VMEM(x.shape, x.dtype) for x in scratch],
        cost_estimate=pl.CostEstimate(flops=flops, bytes_accessed=held, transcendentals=0),
        compiler_params=pltpu.CompilerParams(vmem_limit_bytes=mib * 1024 * 1024),
    )(*scalars, *args)


def sds(shape, dtype):
    return jax.ShapeDtypeStruct(shape, dtype)


def adj_one_kernel(me, blocks, counts, mask, out, deg, acc, held, packed, came, gone):
    my = me[0] >> 3
    loads = [pltpu.make_async_copy(mask.at[b], held.at[b], came.at[b]) for b in range(2)]
    for load in loads:
        load.start()
    acc[...] = jnp.zeros_like(acc)
    lane = lax.broadcasted_iota(jnp.int32, (BLK, BLK), 1)
    for b in range(2):
        loads[b].wait()

        def step(k, total, b=b):
            o = blocks[b, k]
            rel = (o & 7) * NY + ((my - (o >> 3)) & 3)
            m = jnp.where(lane < counts[0, o], held[b, k], 0).astype(F32)
            acc[rel, b * BLK : (b + 1) * BLK, :] += m
            return total + m

        total = lax.fori_loop(0, NB1, step, jnp.zeros((BLK, BLK), F32), unroll=4)
        deg[b * BLK : (b + 1) * BLK, :] = jnp.maximum(jnp.sum(total, axis=1, keepdims=True), 1.0)
    stores = []
    for z in range(NZ):
        for dy in range(NY):
            packed[z, :, dy * BLK : (dy + 1) * BLK] = acc[z * NY + dy].astype(BF)
        stores.append(pltpu.make_async_copy(packed.at[z], out.at[z], gone.at[z]))
        stores[z].start()
    for store in stores:
        store.wait()


def adj_two_kernel(me, blocks, mask, out, deg, acc):
    mz = me[0] & 7
    acc[...] = jnp.zeros_like(acc)

    def step(k, total):
        c = blocks[0, k]
        o = c >> 1
        rel = (o >> 3) * 16 + ((mz - (o & 7)) & 7) * 2 + (c & 1)
        m = mask[0, k].astype(F32)
        acc[rel] += m
        return total + m

    total = lax.fori_loop(0, NB2, step, jnp.zeros((BLK, BLK), F32), unroll=4)
    deg[...] = jnp.maximum(jnp.sum(total, axis=1, keepdims=True), 1.0)
    for y in range(NY):
        for t in range(16):
            out[y, :, t * BLK : (t + 1) * BLK] = acc[y * 16 + t].astype(BF)


def pick_kernel(js, me, ids, table, *outs):
    my, mz = me[0] >> 3, me[0] & 7
    iota = lax.broadcasted_iota(jnp.int32, (BLK, HID), 1).astype(F32)
    for dy in range(NY):
        hots = []
        for j in js:
            r = ((my + dy) & 3) * NZ + ((mz + j) & 7)
            col = jnp.broadcast_to(ids[pl.ds(r, 1), :].astype(F32), (BLK, BLK)).T
            wide = jnp.concatenate([col] * (HID // BLK), axis=1)
            hots.append(jnp.where(wide == iota, 1.0, 0.0).astype(BF))
        hot = jnp.concatenate(hots, axis=0) if len(hots) > 1 else hots[0]
        outs[dy][...] = jnp.dot(hot, table[...], preferred_element_type=F32).astype(BF)


def local_kernel(js, me, adj, *refs):
    rows, outs = refs[:NY], list(refs[NY:])
    for t, j in enumerate(js):
        x = jnp.concatenate([r[t * BLK : (t + 1) * BLK, :] for r in rows], axis=0)
        s = jnp.dot(adj[((me[0] & 7) + j) & 7], x, preferred_element_type=F32)
        if j == 4:
            outs.pop(0)[...] = s[:, :HALF].astype(BF)
            outs.pop(0)[...] = s[:, HALF:].astype(BF)
        else:
            outs.pop(0)[...] = s


def first_add_kernel(p, q, r, l, right, left):
    right[:, :HALF] = (p[:, :HALF] + r[...].astype(F32)).astype(BF)
    right[:, HALF:] = p[:, HALF:].astype(BF)
    left[:, :HALF] = q[:, :HALF].astype(BF)
    left[:, HALF:] = (q[:, HALF:] + l[...].astype(F32)).astype(BF)


def add_kernel(p, q, r, l, right, left):
    right[...] = (p[...] + r[...].astype(F32)).astype(BF)
    left[...] = (q[...] + l[...].astype(F32)).astype(BF)


def pre_kernel(here, right, left, deg, own, w_neigh, pre, pre16, stats):
    s = here[...] + right[...].astype(F32) + left[...].astype(F32)
    high = s.astype(BF)
    low = (s - high.astype(F32)).astype(BF)
    both = jnp.dot(jnp.concatenate([high, low], axis=0), w_neigh[...], preferred_element_type=F32)
    p = own[...] + (both[: 2 * BLK] + both[2 * BLK :]) / deg[...]
    pre[...] = p
    pre16[...] = p.astype(BF)
    stats[0:1, :] = jnp.sum(p, axis=0, keepdims=True)
    stats[1:2, :] = jnp.sum(p * p, axis=0, keepdims=True)


def norm_terms(stats, gain, shift):
    mean = stats[0:1, :] / ROWS
    var = stats[1:2, :] / ROWS - mean * mean
    scale = gain[...] / jnp.sqrt(var + EPS)
    return scale, shift[...] - scale * mean


def states(p, scale, offset):
    return jnp.maximum(p.astype(F32) * scale + offset, 0.0).astype(BF)


def peers_kernel(stats, gain, shift, adj, b0, b1, b2, b3, b5, b6, b7, acc):
    scale, offset = norm_terms(stats, gain, shift)
    for n, (r, b) in enumerate(((0, b0), (1, b1), (7, b7), (2, b2), (6, b6), (3, b3), (5, b5))):
        h = states(b[...], scale, offset)
        m = jnp.concatenate([adj[y, :, r * 256 : (r + 1) * 256] for y in range(NY)], axis=0)
        term = jnp.dot(m, h, preferred_element_type=F32)
        if n == 0:
            acc[...] = term
        else:
            acc[...] += term


def own_kernel(stats, gain, shift, pre, w_self, bias, own):
    scale, offset = norm_terms(stats, gain, shift)
    h = states(pre[:BLK, :], scale, offset)
    own[...] = jnp.dot(h, w_self[...], preferred_element_type=F32) + bias[...]


def last_peers_kernel(me, stats, gain, shift, adj, b4a, b4b, acc, *outs):
    my = me[0] >> 3
    scale, offset = norm_terms(stats, gain, shift)
    h = jnp.concatenate([states(b4a[...], scale, offset), states(b4b[...], scale, offset)], axis=0)
    for dy, out in enumerate(outs):
        y = (my + dy) & 3
        s = jnp.dot(adj[y, :, 1024:1280], h, preferred_element_type=F32)
        s = s + acc[pl.ds(pl.multiple_of(y * BLK, BLK), BLK), :]
        out[...] = s.astype(out.dtype)


def out_kernel(own, p0, p1, p2, p3, deg, w, out):
    s = p0[...] + p1[...].astype(F32) + p2[...].astype(F32) + p3[...].astype(F32)
    n = (s / deg[...]).astype(BF)
    out[...] = (own[...] + jnp.dot(n, w[...], preferred_element_type=F32)).astype(BF)


def along_y(x, k):
    return lax.ppermute(x, "cache", [(y * NZ + z, (y + k) % NY * NZ + z) for y in range(NY) for z in range(NZ)])


def along_z(x, k):
    return lax.ppermute(x, "cache", [(y * NZ + z, y * NZ + (z + k) % NZ) for y in range(NY) for z in range(NZ)])


def after(xs, *first):
    return list(lax.optimization_barrier((*xs, *first))[: len(xs)])


def body(
    feature_rows,
    request_ids,
    request_counts,
    self_ids,
    blocks_one,
    mask_one,
    blocks_two,
    mask_two,
    w1_self,
    w1_neigh,
    w2_self,
    w2_neigh,
    bn_gain,
    bn_shift,
    bias_two,
):
    me = lax.axis_index("cache").astype(jnp.int32).reshape(1)
    gain, shift, bias = (v.reshape(1, HID) for v in (bn_gain, bn_shift, bias_two))

    asked = lax.all_to_all(request_ids, "cache", split_axis=0, concat_axis=0, tiled=True)

    adj, deg_one = pl.pallas_call(
        adj_one_kernel,
        out_shape=[sds((NZ, 2 * BLK, NY * BLK), BF), sds((2 * BLK, 1), F32)],
        in_specs=[SM, SM, SM, HB],
        out_specs=[HB, VM],
        scratch_shapes=[
            pltpu.VMEM((NZ * NY, 2 * BLK, BLK), F32),
            pltpu.VMEM((2, NB1, BLK, BLK), jnp.int32),
            pltpu.VMEM((NZ, 2 * BLK, NY * BLK), BF),
            pltpu.SemaphoreType.DMA((2,)),
            pltpu.SemaphoreType.DMA((NZ,)),
        ],
        cost_estimate=pl.CostEstimate(flops=1 << 22, bytes_accessed=4 << 20, transcendentals=0),
        compiler_params=pltpu.CompilerParams(vmem_limit_bytes=60 << 20),
    )(me, blocks_one, request_counts, mask_one)
    rings = [[y * NZ + z for z in range(NZ)] for y in range(NY)]
    adj = lax.all_to_all(adj, "cache", split_axis=0, concat_axis=0, tiled=True, axis_index_groups=rings)

    adj_two, deg_two = call(
        adj_two_kernel,
        [sds((NY, BLK, 16 * BLK), BF), sds((BLK, 1), F32)],
        [me, blocks_two],
        [mask_two],
        [sds((NY * 16, BLK, BLK), F32)],
        flops=1 << 22,
    )
    own = jnp.dot(feature_rows[self_ids], w1_self, preferred_element_type=F32)
    rows_here = []
    for n, js in enumerate(CHUNKS):
        if n:
            [asked] = after([asked], rows_here[0][1])
        rows = call(
            functools.partial(pick_kernel, js),
            [sds((len(js) * BLK, FEAT), BF)] * NY,
            [me],
            [asked, feature_rows],
            flops=2 * 4 * len(js) * BLK * 1024 * FEAT,
        )
        rows_here.append([along_y(r, dy) if dy else r for dy, r in enumerate(rows)])

    [adj] = after([adj], own, adj_two)
    terms = []
    for js, rows in zip(CHUNKS, rows_here):
        outs = [sds((2 * BLK, HALF), BF)] * 2 if 4 in js else []
        outs += [sds((2 * BLK, FEAT), F32)] * (len(js) - len(outs) // 2)
        terms += call(
            functools.partial(local_kernel, js), outs, [me], [adj, *rows], flops=2 * len(js) * 256 * 512 * FEAT
        )
    right, left = along_z(terms[0], 1), along_z(terms[1], -1)
    for n in range(3):
        right, left = call(
            add_kernel if n else first_add_kernel,
            [sds((2 * BLK, FEAT), BF)] * 2,
            [],
            [*terms[2 + 2 * n : 4 + 2 * n], right, left],
            flops=1 << 20,
        )
        if n == 1:
            [adj_two] = after([adj_two], right)
        right, left = along_z(right, 1), along_z(left, -1)

    rings = [[y * NZ + z for y in range(NY)] for z in range(NZ)]
    adj_two = lax.all_to_all(adj_two, "cache", split_axis=0, concat_axis=0, tiled=True, axis_index_groups=rings)

    pre, pre16, stats = call(
        pre_kernel,
        [sds((2 * BLK, HID), F32), sds((2 * BLK, HID), BF), sds((2, HID), F32)],
        [],
        [terms[8], right, left, deg_one, own, w1_neigh],
        flops=4 * 256 * FEAT * HID,
    )

    def add_over(st, axis, *ks):
        n = lax.axis_size(axis)
        return sum((lax.ppermute(st, axis, [(i, i ^ k) for i in range(n)]) for k in ks), st)

    b1, b7 = along_z(pre16, 1), along_z(pre16, -1)
    stats = add_over(stats, "cache", 4)
    b1, b7 = after([b1, b7], stats)
    b2, b6 = along_z(b1, 1), along_z(b7, -1)
    stats = add_over(add_over(stats, "grp", 1), "grp", 2, 4, 6)
    b2, b6 = after([b2, b6], stats, adj_two)
    b3, b5 = along_z(b2, 1), along_z(b6, -1)
    stats = add_over(add_over(stats, "cache", 8, 16, 24), "cache", 1, 2, 3)
    b3, b5 = after([b3, b5], stats)
    far_a = along_z(b3[:BLK], 1)
    far_b = along_z(b5[BLK:], -1)

    [acc] = call(
        peers_kernel,
        [sds((NY * BLK, HID), F32)],
        [],
        [stats, gain, shift, adj_two, pre16, b1, b2, b3, b5, b6, b7],
        flops=2 * 512 * 1792 * HID,
    )
    parts = call(
        last_peers_kernel,
        [sds((BLK, HID), F32)] + [sds((BLK, HID), BF)] * 3,
        [me],
        [stats, gain, shift, adj_two, far_a, far_b, acc],
        flops=2 * 512 * 256 * HID,
    )
    [pre] = after([pre], parts[0])
    [own_out] = call(
        own_kernel,
        [sds((BLK, HID), F32)],
        [],
        [stats, gain, shift, pre, w2_self, bias],
        flops=2 * BLK * HID * HID,
    )
    parts = [along_y(p, dy) if dy else p for dy, p in enumerate(parts)]
    return call(
        out_kernel,
        [sds((BLK, HID), BF)],
        [],
        [own_out, *parts, deg_two, w2_neigh],
        flops=2 * BLK * HID * HID,
    )[0]


def solution(mesh):
    rows = P(("grp", "cache"))
    in_specs = (rows,) * 8 + (P(),) * 7
    return jax.shard_map(body, mesh=mesh, in_specs=in_specs, out_specs=rows, check_vma=False)
```

```python
import functools
import math

import jax
import jax.numpy as jnp
from jax import lax
from jax.experimental import pallas as pl
from jax.experimental.pallas import tpu as pltpu
from jax.sharding import PartitionSpec as P

BLK = 128
FEAT = 768
HID = 1024
NB1 = 16
NB2 = 24
NY = 4
NZ = 8
ROWS = 65536.0
EPS = 1e-05

BF = jnp.bfloat16
F32 = jnp.float32

VM = pl.BlockSpec(memory_space=pltpu.VMEM)
SM = pl.BlockSpec(memory_space=pltpu.SMEM)
HB = pl.BlockSpec(memory_space=pltpu.HBM)

CHUNKS = ((4, 3, 5), (2, 6, 1, 7, 0))
HALF = FEAT // 2


def nbytes_of(x):
    return math.prod(x.shape) * x.dtype.itemsize


def call(kernel, outs, scalars, args, scratch=(), flops=0):
    held = sum(nbytes_of(x) for x in (*args, *outs, *scratch))
    mib = held * 3 // (2 << 20) + 4
    return pl.pallas_call(
        kernel,
        out_shape=outs,
        in_specs=[SM] * len(scalars) + [VM] * len(args),
        out_specs=[VM] * len(outs),
        scratch_shapes=[pltpu.VMEM(x.shape, x.dtype) for x in scratch],
        cost_estimate=pl.CostEstimate(flops=flops, bytes_accessed=held, transcendentals=0),
        compiler_params=pltpu.CompilerParams(vmem_limit_bytes=mib * 1024 * 1024),
    )(*scalars, *args)


def sds(shape, dtype):
    return jax.ShapeDtypeStruct(shape, dtype)


def adj_one_kernel(me, blocks, counts, mask, out, deg, acc, held, packed, came, gone):
    my = me[0] >> 3
    loads = [pltpu.make_async_copy(mask.at[b], held.at[b], came.at[b]) for b in range(2)]
    for load in loads:
        load.start()
    acc[...] = jnp.zeros_like(acc)
    lane = lax.broadcasted_iota(jnp.int32, (BLK, BLK), 1)
    for b in range(2):
        loads[b].wait()

        def step(k, total, b=b):
            o = blocks[b, k]
            rel = (o & 7) * NY + ((my - (o >> 3)) & 3)
            m = jnp.where(lane < counts[0, o], held[b, k], 0).astype(F32)
            acc[rel, b * BLK : (b + 1) * BLK, :] += m
            return total + m

        total = lax.fori_loop(0, NB1, step, jnp.zeros((BLK, BLK), F32), unroll=4)
        deg[b * BLK : (b + 1) * BLK, :] = jnp.maximum(jnp.sum(total, axis=1, keepdims=True), 1.0)
    stores = []
    for z in range(NZ):
        for dy in range(NY):
            packed[z, :, dy * BLK : (dy + 1) * BLK] = acc[z * NY + dy].astype(BF)
        stores.append(pltpu.make_async_copy(packed.at[z], out.at[z], gone.at[z]))
        stores[z].start()
    for store in stores:
        store.wait()


def adj_two_kernel(me, blocks, mask, out, deg, acc):
    mz = me[0] & 7
    acc[...] = jnp.zeros_like(acc)

    def step(k, total):
        c = blocks[0, k]
        o = c >> 1
        rel = (o >> 3) * 16 + ((mz - (o & 7)) & 7) * 2 + (c & 1)
        m = mask[0, k].astype(F32)
        acc[rel] += m
        return total + m

    total = lax.fori_loop(0, NB2, step, jnp.zeros((BLK, BLK), F32), unroll=4)
    deg[...] = jnp.maximum(jnp.sum(total, axis=1, keepdims=True), 1.0)
    for y in range(NY):
        for t in range(16):
            out[y, :, t * BLK : (t + 1) * BLK] = acc[y * 16 + t].astype(BF)


def pick_kernel(js, dy, me, ids, table, out):
    my, mz = me[0] >> 3, me[0] & 7
    iota = lax.broadcasted_iota(jnp.int32, (BLK, HID), 1).astype(F32)
    hots = []
    for j in js:
        r = ((my + dy) & 3) * NZ + ((mz + j) & 7)
        col = jnp.broadcast_to(ids[pl.ds(r, 1), :].astype(F32), (BLK, BLK)).T
        wide = jnp.concatenate([col] * (HID // BLK), axis=1)
        hots.append(jnp.where(wide == iota, 1.0, 0.0).astype(BF))
    hot = jnp.concatenate(hots, axis=0)
    out[...] = jnp.dot(hot, table[...], preferred_element_type=F32).astype(BF)


def local_kernel(js, first, me, adj, *refs):
    rows, outs = refs[:NY], list(refs[NY:])
    for t, j in enumerate(js):
        here = slice((first + t) * BLK, (first + t + 1) * BLK)
        s = jnp.dot(adj[((me[0] & 7) + j) & 7], jnp.concatenate([r[here, :] for r in rows], axis=0), preferred_element_type=F32)
        if j == 4:
            outs.pop(0)[...] = s[:, :HALF].astype(BF)
            outs.pop(0)[...] = s[:, HALF:].astype(BF)
        else:
            outs.pop(0)[...] = s


def first_add_kernel(p, q, r, l, right, left):
    right[:, :HALF] = (p[:, :HALF] + r[...].astype(F32)).astype(BF)
    right[:, HALF:] = p[:, HALF:].astype(BF)
    left[:, :HALF] = q[:, :HALF].astype(BF)
    left[:, HALF:] = (q[:, HALF:] + l[...].astype(F32)).astype(BF)


def add_kernel(p, q, r, l, right, left):
    right[...] = (p[...] + r[...].astype(F32)).astype(BF)
    left[...] = (q[...] + l[...].astype(F32)).astype(BF)


def pre_kernel(here, right, left, deg, own, w_neigh, pre, pre16, stats):
    s = here[...] + right[...].astype(F32) + left[...].astype(F32)
    high = s.astype(BF)
    low = (s - high.astype(F32)).astype(BF)
    both = jnp.dot(jnp.concatenate([high, low], axis=0), w_neigh[...], preferred_element_type=F32)
    p = own[...] + (both[: 2 * BLK] + both[2 * BLK :]) / deg[...]
    pre[...] = p[:BLK]
    pre16[...] = p.astype(BF)
    stats[0:1, :] = jnp.sum(p, axis=0, keepdims=True)
    stats[1:2, :] = jnp.sum(p * p, axis=0, keepdims=True)


def norm_terms(stats, gain, shift):
    mean = stats[0:1, :] / ROWS
    var = stats[1:2, :] / ROWS - mean * mean
    scale = gain[...] / jnp.sqrt(var + EPS)
    return scale, shift[...] - scale * mean


def states(p, scale, offset):
    return jnp.maximum(p.astype(F32) * scale + offset, 0.0).astype(BF)


def peers_kernel(stats, gain, shift, adj, b0, b1, b2, b3, b5, b6, b7, acc):
    scale, offset = norm_terms(stats, gain, shift)
    for n, (r, b) in enumerate(((0, b0), (1, b1), (7, b7), (2, b2), (6, b6), (3, b3), (5, b5))):
        h = states(b[...], scale, offset)
        m = jnp.concatenate([adj[y, :, r * 256 : (r + 1) * 256] for y in range(NY)], axis=0)
        term = jnp.dot(m, h, preferred_element_type=F32)
        if n == 0:
            acc[...] = term
        else:
            acc[...] += term


def own_kernel(stats, gain, shift, pre, w_self, bias, own):
    scale, offset = norm_terms(stats, gain, shift)
    h = states(pre[...], scale, offset)
    own[...] = jnp.dot(h, w_self[...], preferred_element_type=F32) + bias[...]


def last_peers_kernel(me, stats, gain, shift, adj, b4a, b4b, acc, *outs):
    my = me[0] >> 3
    scale, offset = norm_terms(stats, gain, shift)
    h = jnp.concatenate([states(b4a[...], scale, offset), states(b4b[...], scale, offset)], axis=0)
    for dy, out in enumerate(outs):
        y = (my + dy) & 3
        s = jnp.dot(adj[y, :, 1024:1280], h, preferred_element_type=F32)
        s = s + acc[pl.ds(pl.multiple_of(y * BLK, BLK), BLK), :]
        out[...] = s.astype(out.dtype)


def out_kernel(own, p0, p1, p2, p3, deg, w, out):
    s = p0[...] + p1[...].astype(F32) + p2[...].astype(F32) + p3[...].astype(F32)
    n = (s / deg[...]).astype(BF)
    out[...] = (own[...] + jnp.dot(n, w[...], preferred_element_type=F32)).astype(BF)


def along_y(x, k):
    return lax.ppermute(x, "cache", [(y * NZ + z, (y + k) % NY * NZ + z) for y in range(NY) for z in range(NZ)])


def along_z(x, k):
    return lax.ppermute(x, "cache", [(y * NZ + z, y * NZ + (z + k) % NZ) for y in range(NY) for z in range(NZ)])


def after(xs, *first):
    return list(lax.optimization_barrier((*xs, *first))[: len(xs)])


def body(
    feature_rows,
    request_ids,
    request_counts,
    self_ids,
    blocks_one,
    mask_one,
    blocks_two,
    mask_two,
    w1_self,
    w1_neigh,
    w2_self,
    w2_neigh,
    bn_gain,
    bn_shift,
    bias_two,
):
    me = lax.axis_index("cache").astype(jnp.int32).reshape(1)
    gain, shift, bias = (v.reshape(1, HID) for v in (bn_gain, bn_shift, bias_two))

    asked = lax.all_to_all(request_ids, "cache", split_axis=0, concat_axis=0, tiled=True)

    adj, deg_one = pl.pallas_call(
        adj_one_kernel,
        out_shape=[sds((NZ, 2 * BLK, NY * BLK), BF), sds((2 * BLK, 1), F32)],
        in_specs=[SM, SM, SM, HB],
        out_specs=[HB, VM],
        scratch_shapes=[
            pltpu.VMEM((NZ * NY, 2 * BLK, BLK), F32),
            pltpu.VMEM((2, NB1, BLK, BLK), jnp.int32),
            pltpu.VMEM((NZ, 2 * BLK, NY * BLK), BF),
            pltpu.SemaphoreType.DMA((2,)),
            pltpu.SemaphoreType.DMA((NZ,)),
        ],
        cost_estimate=pl.CostEstimate(flops=1 << 22, bytes_accessed=4 << 20, transcendentals=0),
        compiler_params=pltpu.CompilerParams(vmem_limit_bytes=60 << 20),
    )(me, blocks_one, request_counts, mask_one)
    rings = [[y * NZ + z for z in range(NZ)] for y in range(NY)]
    adj = lax.all_to_all(adj, "cache", split_axis=0, concat_axis=0, tiled=True, axis_index_groups=rings)

    adj_two, deg_two = call(
        adj_two_kernel,
        [sds((NY, BLK, 16 * BLK), BF), sds((BLK, 1), F32)],
        [me, blocks_two],
        [mask_two],
        [sds((NY * 16, BLK, BLK), F32)],
        flops=1 << 22,
    )
    own = jnp.dot(feature_rows[self_ids], w1_self, preferred_element_type=F32)
    rows_here = []
    for n, js in enumerate(CHUNKS):
        if n:
            [asked] = after([asked], rows_here[0][1])
        rows = {}
        for dy in (1, 3, 2, 0):
            [rows[dy]] = call(
                functools.partial(pick_kernel, js, dy),
                [sds((len(js) * BLK, FEAT), BF)],
                [me],
                [asked, feature_rows],
                flops=2 * len(js) * BLK * 1024 * FEAT,
            )
        rows = [along_y(rows[dy], dy) if dy else rows[dy] for dy in range(NY)]
        rows_here.append(rows)

    [adj] = after([adj], own, adj_two)
    terms = []
    for js, first, rows in ((CHUNKS[0], 0, rows_here[0]), ((2, 6), 0, rows_here[1]), ((1, 7, 0), 2, rows_here[1])):
        outs = [sds((2 * BLK, HALF), BF)] * 2 if 4 in js else []
        outs += [sds((2 * BLK, FEAT), F32)] * (len(js) - len(outs) // 2)
        terms += call(
            functools.partial(local_kernel, js, first),
            outs,
            [me],
            [adj, *rows],
            flops=2 * len(js) * 256 * 512 * FEAT,
        )
    right, left = along_z(terms[0], 1), along_z(terms[1], -1)
    for n in range(3):
        right, left = call(
            add_kernel if n else first_add_kernel,
            [sds((2 * BLK, FEAT), BF)] * 2,
            [],
            [*terms[2 + 2 * n : 4 + 2 * n], right, left],
            flops=1 << 20,
        )
        if n == 1:
            [adj_two] = after([adj_two], right)
        right, left = along_z(right, 1), along_z(left, -1)

    rings = [[y * NZ + z for y in range(NY)] for z in range(NZ)]
    adj_two = lax.all_to_all(adj_two, "cache", split_axis=0, concat_axis=0, tiled=True, axis_index_groups=rings)

    pre, pre16, stats = call(
        pre_kernel,
        [sds((BLK, HID), F32), sds((2 * BLK, HID), BF), sds((2, HID), F32)],
        [],
        [terms[8], right, left, deg_one, own, w1_neigh],
        flops=4 * 256 * FEAT * HID,
    )

    def add_over(st, axis, *ks):
        n = lax.axis_size(axis)
        return sum((lax.ppermute(st, axis, [(i, i ^ k) for i in range(n)]) for k in ks), st)

    b1, b7 = along_z(pre16, 1), along_z(pre16, -1)
    stats = add_over(add_over(stats, "grp", 1), "grp", 2, 4, 6)
    b1, b7 = after([b1, b7], stats)
    b2, b6 = along_z(b1, 1), along_z(b7, -1)
    stats = add_over(stats, "cache", 1, 2, 3)
    b2, b6 = after([b2, b6], stats, adj_two)
    b3, b5 = along_z(b2, 1), along_z(b6, -1)
    stats = add_over(add_over(stats, "cache", 8, 16, 24), "cache", 4)
    b3, b5 = after([b3, b5], stats)
    far_a = along_z(b3[:BLK], 1)
    far_b = along_z(b5[BLK:], -1)

    [acc] = call(
        peers_kernel,
        [sds((NY * BLK, HID), F32)],
        [],
        [stats, gain, shift, adj_two, pre16, b1, b2, b3, b5, b6, b7],
        flops=2 * 512 * 1792 * HID,
    )
    parts = call(
        last_peers_kernel,
        [sds((BLK, HID), F32)] + [sds((BLK, HID), BF)] * 3,
        [me],
        [stats, gain, shift, adj_two, far_a, far_b, acc],
        flops=2 * 512 * 256 * HID,
    )
    [pre] = after([pre], parts[0])
    [own_out] = call(
        own_kernel,
        [sds((BLK, HID), F32)],
        [],
        [stats, gain, shift, pre, w2_self, bias],
        flops=2 * BLK * HID * HID,
    )
    parts = [along_y(p, dy) if dy else p for dy, p in enumerate(parts)]
    return call(
        out_kernel,
        [sds((BLK, HID), BF)],
        [],
        [own_out, *parts, deg_two, w2_neigh],
        flops=2 * BLK * HID * HID,
    )[0]


def solution(mesh):
    rows = P(("grp", "cache"))
    in_specs = (rows,) * 8 + (P(),) * 7
    return jax.shard_map(body, mesh=mesh, in_specs=in_specs, out_specs=rows, check_vma=False)
```

```python
import functools
import math

import jax
import jax.numpy as jnp
from jax import lax
from jax.experimental import pallas as pl
from jax.experimental.pallas import tpu as pltpu
from jax.sharding import PartitionSpec as P

BLK = 128
FEAT = 768
HID = 1024
NB1 = 16
NB2 = 24
NY = 4
NZ = 8
ROWS = 65536.0
EPS = 1e-05

BF = jnp.bfloat16
F32 = jnp.float32

VM = pl.BlockSpec(memory_space=pltpu.VMEM)
SM = pl.BlockSpec(memory_space=pltpu.SMEM)
HB = pl.BlockSpec(memory_space=pltpu.HBM)

CHUNKS = ((4, 3, 5), (2, 6, 1, 7, 0))
HALF = FEAT // 2


def nbytes_of(x):
    return math.prod(x.shape) * x.dtype.itemsize


def call(kernel, outs, scalars, args, scratch=(), flops=0):
    held = sum(nbytes_of(x) for x in (*args, *outs, *scratch))
    mib = held * 3 // (2 << 20) + 4
    return pl.pallas_call(
        kernel,
        out_shape=outs,
        in_specs=[SM] * len(scalars) + [VM] * len(args),
        out_specs=[VM] * len(outs),
        scratch_shapes=[pltpu.VMEM(x.shape, x.dtype) for x in scratch],
        cost_estimate=pl.CostEstimate(flops=flops, bytes_accessed=held, transcendentals=0),
        compiler_params=pltpu.CompilerParams(vmem_limit_bytes=mib * 1024 * 1024),
    )(*scalars, *args)


def sds(shape, dtype):
    return jax.ShapeDtypeStruct(shape, dtype)


def adj_one_kernel(me, blocks, counts, mask, out, deg, acc, held, packed, came, gone):
    my = me[0] >> 3
    loads = [pltpu.make_async_copy(mask.at[b], held.at[b], came.at[b]) for b in range(2)]
    for load in loads:
        load.start()
    acc[...] = jnp.zeros_like(acc)
    lane = lax.broadcasted_iota(jnp.int32, (BLK, BLK), 1)
    for b in range(2):
        loads[b].wait()

        def step(k, total, b=b):
            o = blocks[b, k]
            rel = (o & 7) * NY + ((my - (o >> 3)) & 3)
            m = jnp.where(lane < counts[0, o], held[b, k], 0).astype(F32)
            acc[rel, b * BLK : (b + 1) * BLK, :] += m
            return total + m

        total = lax.fori_loop(0, NB1, step, jnp.zeros((BLK, BLK), F32), unroll=4)
        deg[b * BLK : (b + 1) * BLK, :] = jnp.maximum(jnp.sum(total, axis=1, keepdims=True), 1.0)
    stores = []
    for z in range(NZ):
        for dy in range(NY):
            packed[z, :, dy * BLK : (dy + 1) * BLK] = acc[z * NY + dy].astype(BF)
        stores.append(pltpu.make_async_copy(packed.at[z], out.at[z], gone.at[z]))
        stores[z].start()
    for store in stores:
        store.wait()


def adj_two_kernel(me, blocks, mask, out, deg, acc):
    mz = me[0] & 7
    acc[...] = jnp.zeros_like(acc)

    def step(k, total):
        c = blocks[0, k]
        o = c >> 1
        rel = (o >> 3) * 16 + ((mz - (o & 7)) & 7) * 2 + (c & 1)
        m = mask[0, k].astype(F32)
        acc[rel] += m
        return total + m

    total = lax.fori_loop(0, NB2, step, jnp.zeros((BLK, BLK), F32), unroll=4)
    deg[...] = jnp.maximum(jnp.sum(total, axis=1, keepdims=True), 1.0)
    for y in range(NY):
        for t in range(16):
            out[y, :, t * BLK : (t + 1) * BLK] = acc[y * 16 + t].astype(BF)


def pick_kernel(js, dy, me, ids, table, out):
    my, mz = me[0] >> 3, me[0] & 7
    iota = lax.broadcasted_iota(jnp.int32, (BLK, HID), 1).astype(F32)
    hots = []
    for j in js:
        r = ((my + dy) & 3) * NZ + ((mz + j) & 7)
        col = jnp.broadcast_to(ids[pl.ds(r, 1), :].astype(F32), (BLK, BLK)).T
        wide = jnp.concatenate([col] * (HID // BLK), axis=1)
        hots.append(jnp.where(wide == iota, 1.0, 0.0).astype(BF))
    hot = jnp.concatenate(hots, axis=0)
    out[...] = jnp.dot(hot, table[...], preferred_element_type=F32).astype(BF)


def local_kernel(js, first, me, adj, *refs):
    rows, outs = refs[:NY], list(refs[NY:])
    for t, j in enumerate(js):
        here = slice((first + t) * BLK, (first + t + 1) * BLK)
        s = jnp.dot(adj[((me[0] & 7) + j) & 7], jnp.concatenate([r[here, :] for r in rows], axis=0), preferred_element_type=F32)
        if j == 4:
            outs.pop(0)[...] = s[:, :HALF].astype(BF)
            outs.pop(0)[...] = s[:, HALF:].astype(BF)
        else:
            outs.pop(0)[...] = s


def first_add_kernel(p, q, r, l, right, left):
    right[:, :HALF] = (p[:, :HALF] + r[...].astype(F32)).astype(BF)
    right[:, HALF:] = p[:, HALF:].astype(BF)
    left[:, :HALF] = q[:, :HALF].astype(BF)
    left[:, HALF:] = (q[:, HALF:] + l[...].astype(F32)).astype(BF)


def add_kernel(p, q, r, l, right, left):
    right[...] = (p[...] + r[...].astype(F32)).astype(BF)
    left[...] = (q[...] + l[...].astype(F32)).astype(BF)


def pre_kernel(here, right, left, deg, own, w_neigh, pre, pre16, stats):
    s = here[...] + right[...].astype(F32) + left[...].astype(F32)
    high = s.astype(BF)
    low = (s - high.astype(F32)).astype(BF)
    both = jnp.dot(jnp.concatenate([high, low], axis=0), w_neigh[...], preferred_element_type=F32)
    p = own[...] + (both[: 2 * BLK] + both[2 * BLK :]) / deg[...]
    pre[...] = p[:BLK]
    pre16[...] = p.astype(BF)
    stats[0:1, :] = jnp.sum(p, axis=0, keepdims=True)
    stats[1:2, :] = jnp.sum(p * p, axis=0, keepdims=True)


def norm_terms(stats, gain, shift):
    mean = stats[0:1, :] / ROWS
    var = stats[1:2, :] / ROWS - mean * mean
    scale = gain[...] / jnp.sqrt(var + EPS)
    return scale, shift[...] - scale * mean


def states(p, scale, offset):
    return jnp.maximum(p.astype(F32) * scale + offset, 0.0).astype(BF)


def peers_kernel(stats, gain, shift, adj, b0, b1, b2, b3, b5, b6, b7, acc):
    scale, offset = norm_terms(stats, gain, shift)
    for n, (r, b) in enumerate(((0, b0), (1, b1), (7, b7), (2, b2), (6, b6), (3, b3), (5, b5))):
        h = states(b[...], scale, offset)
        m = jnp.concatenate([adj[y, :, r * 256 : (r + 1) * 256] for y in range(NY)], axis=0)
        term = jnp.dot(m, h, preferred_element_type=F32)
        if n == 0:
            acc[...] = term
        else:
            acc[...] += term


def own_kernel(stats, gain, shift, pre, w_self, bias, own):
    scale, offset = norm_terms(stats, gain, shift)
    h = states(pre[...], scale, offset)
    own[...] = jnp.dot(h, w_self[...], preferred_element_type=F32) + bias[...]


def last_peers_kernel(me, stats, gain, shift, adj, b4a, b4b, acc, *outs):
    my = me[0] >> 3
    scale, offset = norm_terms(stats, gain, shift)
    h = jnp.concatenate([states(b4a[...], scale, offset), states(b4b[...], scale, offset)], axis=0)
    for dy, out in enumerate(outs):
        y = (my + dy) & 3
        s = jnp.dot(adj[y, :, 1024:1280], h, preferred_element_type=F32)
        s = s + acc[pl.ds(pl.multiple_of(y * BLK, BLK), BLK), :]
        out[...] = s.astype(out.dtype)


def out_kernel(own, p0, p1, p2, p3, deg, w, out):
    s = p0[...] + p1[...].astype(F32) + p2[...].astype(F32) + p3[...].astype(F32)
    n = (s / deg[...]).astype(BF)
    out[...] = (own[...] + jnp.dot(n, w[...], preferred_element_type=F32)).astype(BF)


def along_y(x, k):
    return lax.ppermute(x, "cache", [(y * NZ + z, (y + k) % NY * NZ + z) for y in range(NY) for z in range(NZ)])


def along_z(x, k):
    return lax.ppermute(x, "cache", [(y * NZ + z, y * NZ + (z + k) % NZ) for y in range(NY) for z in range(NZ)])


def after(xs, *first):
    return list(lax.optimization_barrier((*xs, *first))[: len(xs)])


def body(
    feature_rows,
    request_ids,
    request_counts,
    self_ids,
    blocks_one,
    mask_one,
    blocks_two,
    mask_two,
    w1_self,
    w1_neigh,
    w2_self,
    w2_neigh,
    bn_gain,
    bn_shift,
    bias_two,
):
    me = lax.axis_index("cache").astype(jnp.int32).reshape(1)
    gain, shift, bias = (v.reshape(1, HID) for v in (bn_gain, bn_shift, bias_two))

    asked = lax.all_to_all(request_ids, "cache", split_axis=0, concat_axis=0, tiled=True)

    adj, deg_one = pl.pallas_call(
        adj_one_kernel,
        out_shape=[sds((NZ, 2 * BLK, NY * BLK), BF), sds((2 * BLK, 1), F32)],
        in_specs=[SM, SM, SM, HB],
        out_specs=[HB, VM],
        scratch_shapes=[
            pltpu.VMEM((NZ * NY, 2 * BLK, BLK), F32),
            pltpu.VMEM((2, NB1, BLK, BLK), jnp.int32),
            pltpu.VMEM((NZ, 2 * BLK, NY * BLK), BF),
            pltpu.SemaphoreType.DMA((2,)),
            pltpu.SemaphoreType.DMA((NZ,)),
        ],
        cost_estimate=pl.CostEstimate(flops=1 << 22, bytes_accessed=4 << 20, transcendentals=0),
        compiler_params=pltpu.CompilerParams(vmem_limit_bytes=60 << 20),
    )(me, blocks_one, request_counts, mask_one)
    rings = [[y * NZ + z for z in range(NZ)] for y in range(NY)]
    adj = lax.all_to_all(adj, "cache", split_axis=0, concat_axis=0, tiled=True, axis_index_groups=rings)

    adj_two, deg_two = call(
        adj_two_kernel,
        [sds((NY, BLK, 16 * BLK), BF), sds((BLK, 1), F32)],
        [me, blocks_two],
        [mask_two],
        [sds((NY * 16, BLK, BLK), F32)],
        flops=1 << 22,
    )
    own = jnp.dot(feature_rows[self_ids], w1_self, preferred_element_type=F32)
    rows_here = []
    for n, js in enumerate(CHUNKS):
        if n:
            [asked] = after([asked], rows_here[0][1])
        rows = {}
        for dy in (1, 3, 2, 0):
            [rows[dy]] = call(
                functools.partial(pick_kernel, js, dy),
                [sds((len(js) * BLK, FEAT), BF)],
                [me],
                [asked, feature_rows],
                flops=2 * len(js) * BLK * 1024 * FEAT,
            )
        rows = [along_y(rows[dy], dy) if dy else rows[dy] for dy in range(NY)]
        rows_here.append(rows)

    [adj] = after([adj], own, adj_two)
    terms = []
    for js, first, rows in ((CHUNKS[0], 0, rows_here[0]), ((2, 6), 0, rows_here[1]), ((1, 7, 0), 2, rows_here[1])):
        outs = [sds((2 * BLK, HALF), BF)] * 2 if 4 in js else []
        outs += [sds((2 * BLK, FEAT), F32)] * (len(js) - len(outs) // 2)
        terms += call(
            functools.partial(local_kernel, js, first),
            outs,
            [me],
            [adj, *rows],
            flops=2 * len(js) * 256 * 512 * FEAT,
        )
    right, left = along_z(terms[0], 1), along_z(terms[1], -1)
    for n in range(3):
        right, left = call(
            add_kernel if n else first_add_kernel,
            [sds((2 * BLK, FEAT), BF)] * 2,
            [],
            [*terms[2 + 2 * n : 4 + 2 * n], right, left],
            flops=1 << 20,
        )
        if n == 1:
            [adj_two] = after([adj_two], right)
        right, left = along_z(right, 1), along_z(left, -1)

    rings = [[y * NZ + z for y in range(NY)] for z in range(NZ)]
    adj_two = lax.all_to_all(adj_two, "cache", split_axis=0, concat_axis=0, tiled=True, axis_index_groups=rings)

    pre, pre16, stats = call(
        pre_kernel,
        [sds((BLK, HID), F32), sds((2 * BLK, HID), BF), sds((2, HID), F32)],
        [],
        [terms[8], right, left, deg_one, own, w1_neigh],
        flops=4 * 256 * FEAT * HID,
    )

    def add_over(st, axis, *ks):
        n = lax.axis_size(axis)
        return sum((lax.ppermute(st, axis, [(i, i ^ k) for i in range(n)]) for k in ks), st)

    b1, b7 = along_z(pre16, 1), along_z(pre16, -1)
    stats = add_over(stats, "grp", 2, 4, 6)
    b1, b7 = after([b1, b7], stats)
    b2, b6 = along_z(b1, 1), along_z(b7, -1)
    stats = add_over(stats, "cache", 8, 16, 24)
    b2, b6, stats = after([b2, b6, stats], stats, adj_two)
    b3, b5 = along_z(b2, 1), along_z(b6, -1)
    stats = jnp.broadcast_to(add_over(stats, "grp", 1), (NZ, 2, HID))
    rings = [[y * NZ + z for z in range(NZ)] for y in range(NY)]
    stats = lax.all_to_all(stats, "cache", split_axis=0, concat_axis=0, tiled=True, axis_index_groups=rings)
    stats = jnp.sum(stats, axis=0)
    far_a = along_z(b3[:BLK], 1)
    far_b = along_z(b5[BLK:], -1)

    [acc] = call(
        peers_kernel,
        [sds((NY * BLK, HID), F32)],
        [],
        [stats, gain, shift, adj_two, pre16, b1, b2, b3, b5, b6, b7],
        flops=2 * 512 * 1792 * HID,
    )
    parts = call(
        last_peers_kernel,
        [sds((BLK, HID), F32)] + [sds((BLK, HID), BF)] * 3,
        [me],
        [stats, gain, shift, adj_two, far_a, far_b, acc],
        flops=2 * 512 * 256 * HID,
    )
    [pre] = after([pre], parts[0])
    [own_out] = call(
        own_kernel,
        [sds((BLK, HID), F32)],
        [],
        [stats, gain, shift, pre, w2_self, bias],
        flops=2 * BLK * HID * HID,
    )
    parts = [along_y(p, dy) if dy else p for dy, p in enumerate(parts)]
    return call(
        out_kernel,
        [sds((BLK, HID), BF)],
        [],
        [own_out, *parts, deg_two, w2_neigh],
        flops=2 * BLK * HID * HID,
    )[0]


def solution(mesh):
    rows = P(("grp", "cache"))
    in_specs = (rows,) * 8 + (P(),) * 7
    return jax.shard_map(body, mesh=mesh, in_specs=in_specs, out_specs=rows, check_vma=False)
```

```python
import functools
import math

import jax
import jax.numpy as jnp
from jax import lax
from jax.experimental import pallas as pl
from jax.experimental.pallas import tpu as pltpu
from jax.sharding import PartitionSpec as P

BLK = 128
FEAT = 768
HID = 1024
NB1 = 16
NB2 = 24
NY = 4
NZ = 8
ROWS = 65536.0
EPS = 1e-05

BF = jnp.bfloat16
F32 = jnp.float32

VM = pl.BlockSpec(memory_space=pltpu.VMEM)
SM = pl.BlockSpec(memory_space=pltpu.SMEM)
HB = pl.BlockSpec(memory_space=pltpu.HBM)

CHUNKS = ((4, 3, 5), (2, 6, 1, 7, 0))
HALF = FEAT // 2


def nbytes_of(x):
    return math.prod(x.shape) * x.dtype.itemsize


def call(kernel, outs, scalars, args, scratch=(), flops=0):
    held = sum(nbytes_of(x) for x in (*args, *outs, *scratch))
    mib = held * 3 // (2 << 20) + 4
    return pl.pallas_call(
        kernel,
        out_shape=outs,
        in_specs=[SM] * len(scalars) + [VM] * len(args),
        out_specs=[VM] * len(outs),
        scratch_shapes=[pltpu.VMEM(x.shape, x.dtype) for x in scratch],
        cost_estimate=pl.CostEstimate(flops=flops, bytes_accessed=held, transcendentals=0),
        compiler_params=pltpu.CompilerParams(vmem_limit_bytes=mib * 1024 * 1024),
    )(*scalars, *args)


def sds(shape, dtype):
    return jax.ShapeDtypeStruct(shape, dtype)


def adj_one_kernel(me, blocks, counts, mask, out, deg, acc, held, packed, came, gone):
    my = me[0] >> 3
    loads = [pltpu.make_async_copy(mask.at[b], held.at[b], came.at[b]) for b in range(2)]
    for load in loads:
        load.start()
    acc[...] = jnp.zeros_like(acc)
    lane = lax.broadcasted_iota(jnp.int32, (BLK, BLK), 1)
    for b in range(2):
        loads[b].wait()

        def step(k, total, b=b):
            o = blocks[b, k]
            rel = (o & 7) * NY + ((my - (o >> 3)) & 3)
            m = jnp.where(lane < counts[0, o], held[b, k], 0).astype(F32)
            acc[rel, b * BLK : (b + 1) * BLK, :] += m
            return total + m

        total = lax.fori_loop(0, NB1, step, jnp.zeros((BLK, BLK), F32), unroll=4)
        deg[b * BLK : (b + 1) * BLK, :] = jnp.maximum(jnp.sum(total, axis=1, keepdims=True), 1.0)
    stores = []
    for z in range(NZ):
        for dy in range(NY):
            packed[z, :, dy * BLK : (dy + 1) * BLK] = acc[z * NY + dy].astype(BF)
        stores.append(pltpu.make_async_copy(packed.at[z], out.at[z], gone.at[z]))
        stores[z].start()
    for store in stores:
        store.wait()


def adj_two_kernel(me, blocks, mask, out, deg, acc):
    mz = me[0] & 7
    acc[...] = jnp.zeros_like(acc)

    def step(k, total):
        c = blocks[0, k]
        o = c >> 1
        rel = (o >> 3) * 16 + ((mz - (o & 7)) & 7) * 2 + (c & 1)
        m = mask[0, k].astype(F32)
        acc[rel] += m
        return total + m

    total = lax.fori_loop(0, NB2, step, jnp.zeros((BLK, BLK), F32), unroll=4)
    deg[...] = jnp.maximum(jnp.sum(total, axis=1, keepdims=True), 1.0)
    for y in range(NY):
        for t in range(16):
            out[y, :, t * BLK : (t + 1) * BLK] = acc[y * 16 + t].astype(BF)


def pick_kernel(js, dy, me, ids, table, out):
    my, mz = me[0] >> 3, me[0] & 7
    iota = lax.broadcasted_iota(jnp.int32, (BLK, HID), 1).astype(F32)
    hots = []
    for j in js:
        r = ((my + dy) & 3) * NZ + ((mz + j) & 7)
        col = jnp.broadcast_to(ids[pl.ds(r, 1), :].astype(F32), (BLK, BLK)).T
        wide = jnp.concatenate([col] * (HID // BLK), axis=1)
        hots.append(jnp.where(wide == iota, 1.0, 0.0).astype(BF))
    hot = jnp.concatenate(hots, axis=0)
    out[...] = jnp.dot(hot, table[...], preferred_element_type=F32).astype(BF)


def local_kernel(js, first, me, adj, *refs):
    rows, outs = refs[:NY], list(refs[NY:])
    for t, j in enumerate(js):
        here = slice((first + t) * BLK, (first + t + 1) * BLK)
        s = jnp.dot(adj[((me[0] & 7) + j) & 7], jnp.concatenate([r[here, :] for r in rows], axis=0), preferred_element_type=F32)
        if j == 4:
            outs.pop(0)[...] = s[:, :HALF].astype(BF)
            outs.pop(0)[...] = s[:, HALF:].astype(BF)
        else:
            outs.pop(0)[...] = s


def first_add_kernel(p, q, r, l, right, left):
    right[:, :HALF] = (p[:, :HALF] + r[...].astype(F32)).astype(BF)
    right[:, HALF:] = p[:, HALF:].astype(BF)
    left[:, :HALF] = q[:, :HALF].astype(BF)
    left[:, HALF:] = (q[:, HALF:] + l[...].astype(F32)).astype(BF)


def add_kernel(p, q, r, l, right, left):
    right[...] = (p[...] + r[...].astype(F32)).astype(BF)
    left[...] = (q[...] + l[...].astype(F32)).astype(BF)


def pre_kernel(here, right, left, deg, own, w_neigh, pre, pre16, stats):
    s = here[...] + right[...].astype(F32) + left[...].astype(F32)
    high = s.astype(BF)
    low = (s - high.astype(F32)).astype(BF)
    both = jnp.dot(jnp.concatenate([high, low], axis=0), w_neigh[...], preferred_element_type=F32)
    p = own[...] + (both[: 2 * BLK] + both[2 * BLK :]) / deg[...]
    pre[...] = p[:BLK]
    pre16[...] = p.astype(BF)
    stats[0:1, :] = jnp.sum(p, axis=0, keepdims=True)
    stats[1:2, :] = jnp.sum(p * p, axis=0, keepdims=True)


def norm_terms(stats, gain, shift):
    total = jnp.sum(stats[...], axis=0)
    mean = total[0:1, :] / ROWS
    var = total[1:2, :] / ROWS - mean * mean
    scale = gain[...] / jnp.sqrt(var + EPS)
    return scale, shift[...] - scale * mean


def states(p, scale, offset):
    return jnp.maximum(p.astype(F32) * scale + offset, 0.0).astype(BF)


def peers_kernel(stats, gain, shift, adj, b0, b1, b2, b3, b5, b6, b7, acc):
    scale, offset = norm_terms(stats, gain, shift)
    for n, (r, b) in enumerate(((0, b0), (1, b1), (7, b7), (2, b2), (6, b6), (3, b3), (5, b5))):
        h = states(b[...], scale, offset)
        m = jnp.concatenate([adj[y, :, r * 256 : (r + 1) * 256] for y in range(NY)], axis=0)
        term = jnp.dot(m, h, preferred_element_type=F32)
        if n == 0:
            acc[...] = term
        else:
            acc[...] += term


def own_kernel(stats, gain, shift, pre, w_self, bias, own):
    scale, offset = norm_terms(stats, gain, shift)
    h = states(pre[...], scale, offset)
    own[...] = jnp.dot(h, w_self[...], preferred_element_type=F32) + bias[...]


def last_peers_kernel(me, stats, gain, shift, adj, b4a, b4b, acc, *outs):
    my = me[0] >> 3
    scale, offset = norm_terms(stats, gain, shift)
    h = jnp.concatenate([states(b4a[...], scale, offset), states(b4b[...], scale, offset)], axis=0)
    for dy, out in enumerate(outs):
        y = (my + dy) & 3
        s = jnp.dot(adj[y, :, 1024:1280], h, preferred_element_type=F32)
        s = s + acc[pl.ds(pl.multiple_of(y * BLK, BLK), BLK), :]
        out[...] = s.astype(out.dtype)


def out_kernel(own, p0, p1, p2, p3, deg, w, out):
    s = p0[...] + p1[...].astype(F32) + p2[...].astype(F32) + p3[...].astype(F32)
    n = (s / deg[...]).astype(BF)
    out[...] = (own[...] + jnp.dot(n, w[...], preferred_element_type=F32)).astype(BF)


def along_y(x, k):
    return lax.ppermute(x, "cache", [(y * NZ + z, (y + k) % NY * NZ + z) for y in range(NY) for z in range(NZ)])


def along_z(x, k):
    return lax.ppermute(x, "cache", [(y * NZ + z, y * NZ + (z + k) % NZ) for y in range(NY) for z in range(NZ)])


def after(xs, *first):
    return list(lax.optimization_barrier((*xs, *first))[: len(xs)])


def body(
    feature_rows,
    request_ids,
    request_counts,
    self_ids,
    blocks_one,
    mask_one,
    blocks_two,
    mask_two,
    w1_self,
    w1_neigh,
    w2_self,
    w2_neigh,
    bn_gain,
    bn_shift,
    bias_two,
):
    me = lax.axis_index("cache").astype(jnp.int32).reshape(1)
    gain, shift, bias = (v.reshape(1, HID) for v in (bn_gain, bn_shift, bias_two))

    asked = lax.all_to_all(request_ids, "cache", split_axis=0, concat_axis=0, tiled=True)

    adj, deg_one = pl.pallas_call(
        adj_one_kernel,
        out_shape=[sds((NZ, 2 * BLK, NY * BLK), BF), sds((2 * BLK, 1), F32)],
        in_specs=[SM, SM, SM, HB],
        out_specs=[HB, VM],
        scratch_shapes=[
            pltpu.VMEM((NZ * NY, 2 * BLK, BLK), F32),
            pltpu.VMEM((2, NB1, BLK, BLK), jnp.int32),
            pltpu.VMEM((NZ, 2 * BLK, NY * BLK), BF),
            pltpu.SemaphoreType.DMA((2,)),
            pltpu.SemaphoreType.DMA((NZ,)),
        ],
        cost_estimate=pl.CostEstimate(flops=1 << 22, bytes_accessed=4 << 20, transcendentals=0),
        compiler_params=pltpu.CompilerParams(vmem_limit_bytes=60 << 20),
    )(me, blocks_one, request_counts, mask_one)
    rings = [[y * NZ + z for z in range(NZ)] for y in range(NY)]
    adj = lax.all_to_all(adj, "cache", split_axis=0, concat_axis=0, tiled=True, axis_index_groups=rings)

    adj_two, deg_two = call(
        adj_two_kernel,
        [sds((NY, BLK, 16 * BLK), BF), sds((BLK, 1), F32)],
        [me, blocks_two],
        [mask_two],
        [sds((NY * 16, BLK, BLK), F32)],
        flops=1 << 22,
    )
    own = jnp.dot(feature_rows[self_ids], w1_self, preferred_element_type=F32)
    rows_here = []
    for n, js in enumerate(CHUNKS):
        if n:
            [asked] = after([asked], rows_here[0][1])
        rows = {}
        for dy in (1, 3, 2, 0):
            [rows[dy]] = call(
                functools.partial(pick_kernel, js, dy),
                [sds((len(js) * BLK, FEAT), BF)],
                [me],
                [asked, feature_rows],
                flops=2 * len(js) * BLK * 1024 * FEAT,
            )
        rows = [along_y(rows[dy], dy) if dy else rows[dy] for dy in range(NY)]
        rows_here.append(rows)

    [adj] = after([adj], own, adj_two)
    terms = []
    for js, first, rows in ((CHUNKS[0], 0, rows_here[0]), ((2, 6), 0, rows_here[1]), ((1, 7, 0), 2, rows_here[1])):
        outs = [sds((2 * BLK, HALF), BF)] * 2 if 4 in js else []
        outs += [sds((2 * BLK, FEAT), F32)] * (len(js) - len(outs) // 2)
        terms += call(
            functools.partial(local_kernel, js, first),
            outs,
            [me],
            [adj, *rows],
            flops=2 * len(js) * 256 * 512 * FEAT,
        )
    right, left = along_z(terms[0], 1), along_z(terms[1], -1)
    for n in range(3):
        right, left = call(
            add_kernel if n else first_add_kernel,
            [sds((2 * BLK, FEAT), BF)] * 2,
            [],
            [*terms[2 + 2 * n : 4 + 2 * n], right, left],
            flops=1 << 20,
        )
        if n == 1:
            [adj_two] = after([adj_two], right)
        right, left = along_z(right, 1), along_z(left, -1)

    rings = [[y * NZ + z for y in range(NY)] for z in range(NZ)]
    adj_two = lax.all_to_all(adj_two, "cache", split_axis=0, concat_axis=0, tiled=True, axis_index_groups=rings)

    pre, pre16, stats = call(
        pre_kernel,
        [sds((BLK, HID), F32), sds((2 * BLK, HID), BF), sds((2, HID), F32)],
        [],
        [terms[8], right, left, deg_one, own, w1_neigh],
        flops=4 * 256 * FEAT * HID,
    )

    def add_over(st, axis, *ks):
        n = lax.axis_size(axis)
        return sum((lax.ppermute(st, axis, [(i, i ^ k) for i in range(n)]) for k in ks), st)

    b1, b7 = along_z(pre16, 1), along_z(pre16, -1)
    stats = add_over(stats, "grp", 2, 4, 6)
    b1, b7 = after([b1, b7], stats)
    b2, b6 = along_z(b1, 1), along_z(b7, -1)
    stats = add_over(stats, "cache", 8, 16, 24)
    b2, b6, stats = after([b2, b6, stats], adj_two)
    b3, b5 = along_z(b2, 1), along_z(b6, -1)
    stats = jnp.broadcast_to(add_over(stats, "grp", 1), (NZ, 2, HID))
    rings = [[y * NZ + z for z in range(NZ)] for y in range(NY)]
    stats = lax.all_to_all(stats, "cache", split_axis=0, concat_axis=0, tiled=True, axis_index_groups=rings)
    far_a = along_z(b3[:BLK], 1)
    far_b = along_z(b5[BLK:], -1)

    [acc] = call(
        peers_kernel,
        [sds((NY * BLK, HID), F32)],
        [],
        [stats, gain, shift, adj_two, pre16, b1, b2, b3, b5, b6, b7],
        flops=2 * 512 * 1792 * HID,
    )
    parts = call(
        last_peers_kernel,
        [sds((BLK, HID), F32)] + [sds((BLK, HID), BF)] * 3,
        [me],
        [stats, gain, shift, adj_two, far_a, far_b, acc],
        flops=2 * 512 * 256 * HID,
    )
    [pre] = after([pre], parts[0])
    [own_out] = call(
        own_kernel,
        [sds((BLK, HID), F32)],
        [],
        [stats, gain, shift, pre, w2_self, bias],
        flops=2 * BLK * HID * HID,
    )
    parts = [along_y(p, dy) if dy else p for dy, p in enumerate(parts)]
    return call(
        out_kernel,
        [sds((BLK, HID), BF)],
        [],
        [own_out, *parts, deg_two, w2_neigh],
        flops=2 * BLK * HID * HID,
    )[0]


def solution(mesh):
    rows = P(("grp", "cache"))
    in_specs = (rows,) * 8 + (P(),) * 7
    return jax.shard_map(body, mesh=mesh, in_specs=in_specs, out_specs=rows, check_vma=False)
```
